32 devices in a mesh: gx: 8 (over y, x, core), gy: 4 (over z).
Axes of the slice: x: 2, y: 2, z: 4, core: 2. Of those that a mesh axis runs over, the one named last changes fastest.
Arguments:
- coefficients: float32 [8, 4, 256, 1024], P('gx', 'gy'), may hold values from -6 to 6
- transfer_blocks: float32 [4, 8, 4, 256, 512], P(None, 'gx', 'gy'), may hold values from -0.25 to 0.25
Outputs:
- result_blocks: float32 [8, 4, 256, 1024], P('gx', 'gy')
The draws below stay inside these ranges and needn't reach their ends.
All inputs are finite; a program needn't handle non-finite values.
Results may differ from the reference program's by a relative error of at most 0.0001.
Values sent between devices are 32-bit elements; how exact they have to be, the bound alone decides.
A program may use at most 64 MiB of HBM per device.

```python
import jax
import jax.numpy as jnp
from jax import lax

RANK = 256
NRHS = 1024
LEVELS = 4
BX = 8
BY = 4


def block_levels(rng, shape, split, smallest, high):
    gain = 1.0
    for axis_at, shards_of in split:
        steps = jax.random.uniform(jax.random.fold_in(jax.random.fold_in(rng, 6), axis_at), (shards_of,), jnp.float32, smallest / len(split), high / len(split))
        gain = gain * jnp.repeat(jnp.exp(steps), shape[axis_at] // shards_of).reshape((-1,) + (1,) * (len(shape) - 1 - axis_at))
    return gain


def gaussian(stream_key, shape, deviation, reach, cuts=(), kind=jnp.bfloat16):
    level = block_levels(stream_key, shape, cuts, -0.22, 0.18) if cuts else 1.0
    result = jax.random.normal(stream_key, shape, jnp.float32) * deviation * level
    return jnp.minimum(jnp.maximum(result, -reach), reach).astype(kind)


def setup_inputs(seed: int = 0) -> dict:
    streams_of = jax.random.split(jax.random.key(seed), 3)
    coefficients = gaussian(streams_of[0], (BX, BY, RANK, NRHS), 1.0, 6.0, ((0, 8), (1, 4)), jnp.float32)
    transfer_blocks = gaussian(streams_of[1], (LEVELS, BX, BY, RANK, 2 * RANK), (2 * RANK) ** -0.5, 0.25, ((1, 8), (2, 4)), jnp.float32)
    return dict(coefficients=coefficients, transfer_blocks=transfer_blocks)


def apply_level(state, blocks, axis_number, bit_number):
    block_count = state.shape[axis_number]
    position = jnp.arange(block_count, dtype=jnp.int32)
    partner = jnp.take(state, jnp.bitwise_xor(position, jnp.int32(1 << bit_number)), axis=axis_number)
    upper_bit = jnp.bitwise_and(jnp.right_shift(position, bit_number), 1)
    if axis_number == 0:
        upper_bit = upper_bit.reshape(-1, 1, 1, 1)
    else:
        upper_bit = upper_bit.reshape(1, -1, 1, 1)
    lower_block = jnp.where(upper_bit == 0, state, partner)
    upper_block = jnp.where(upper_bit == 0, partner, state)
    first_term = jnp.einsum("xyrk,xykn->xyrn", blocks[..., :RANK], lower_block, precision=lax.Precision.HIGHEST)
    second_term = jnp.einsum("xyrk,xykn->xyrn", blocks[..., RANK:], upper_block, precision=lax.Precision.HIGHEST)
    return first_term + second_term


def reference(coefficients, transfer_blocks):
    high_top = BX.bit_length() - 2
    low_top = BY.bit_length() - 2
    plan = [(0, high_top), (1, low_top), (0, high_top - 1), (1, low_top - 1)]
    state = coefficients
    for level_number in range(LEVELS):
        axis_number, bit_number = plan[level_number]
        state = apply_level(state, transfer_blocks[level_number], axis_number, bit_number)
    return state
```

```python
import functools

import jax
import jax.numpy as jnp
from jax import lax
from jax.experimental import pallas as pl
from jax.experimental.pallas import tpu as pltpu
from jax.sharding import PartitionSpec as P

MESH = pl.DeviceIdType.MESH
WIDTH = 128
LEAD = 2


def high_low(x):
    high = x.astype(jnp.bfloat16)
    low = (x - high.astype(jnp.float32)).astype(jnp.bfloat16)
    return high, low


def right_side(x):
    high, low = high_low(x)
    return jnp.concatenate([high, low, high], axis=0)


def product(left, x):
    return jnp.dot(left, right_side(x), preferred_element_type=jnp.float32)


def kernel(plan, coef, blocks, out, state, got, raw, left, result,
           coef_sem, raw_sem, out_sem, send_sem, recv_sem):
    levels, chunks, rank, width = state.shape
    position = {"gx": lax.axis_index("gx"), "gy": lax.axis_index("gy")}
    upper, partner = [], []
    for axis, bit in plan:
        at = position[axis]
        one = lax.rem(at // (1 << bit), 2)
        upper.append(one)
        there = at + (1 - 2 * one) * (1 << bit)
        partner.append(
            (there, position["gy"]) if axis == "gx" else (position["gx"], there)
        )

    def columns(c):
        return pl.ds(pl.multiple_of(c * width, width), width)

    def load(c):
        return pltpu.make_async_copy(coef.at[:, columns(c)], state.at[0, c], coef_sem.at[c])

    def load_blocks(l):
        return pltpu.make_async_copy(blocks.at[l], raw.at[l], raw_sem.at[l])

    def send(l, c):
        return pltpu.make_async_remote_copy(
            src_ref=state.at[l, c],
            dst_ref=got.at[l, c],
            send_sem=send_sem.at[l, c],
            recv_sem=recv_sem.at[l, c],
            device_id=partner[l],
            device_id_type=MESH,
        )

    def store(c):
        return pltpu.make_async_copy(result.at[c], out.at[:, columns(c)], out_sem.at[c])

    for c in range(chunks):
        load(c).start()
    for l in range(levels):
        load_blocks(l).start()

    barrier = pltpu.get_barrier_semaphore()
    for l in range(levels):
        pl.semaphore_signal(barrier, inc=1, device_id=partner[l], device_id_type=MESH)
    pl.semaphore_wait(barrier, levels)

    for c in range(chunks):
        load(c).wait()
        send(0, c).start()

    for l in range(levels):
        load_blocks(l).wait()
        for j in range(2):
            half = upper[l] if j == 0 else 1 - upper[l]
            part = raw[l, :, pl.ds(pl.multiple_of(half * rank, rank), rank)]
            high, low = high_low(part)
            left[l, j] = jnp.concatenate([high, high, low], axis=1)

    def stage(l, c):
        own = product(left[l, 0], state[l, c])
        send(l, c).wait_recv()
        new = own + product(left[l, 1], got[l, c])
        if l + 1 < levels:
            state[l + 1, c] = new
            send(l + 1, c).start()
        else:
            result[c] = new
            store(c).start()

    def tick(t, carry):
        for l in range(levels):
            c = t - (0 if l == 0 else LEAD + l - 1)

            @pl.when(jnp.logical_and(c >= 0, c < chunks))
            def _(l=l, c=c):
                stage(l, c)

        return carry

    lax.fori_loop(0, chunks + LEAD + levels - 2, tick, 0)

    def finish(c, carry):
        for l in range(levels):
            send(l, c).wait_send()
        store(c).wait()
        return carry

    lax.fori_loop(0, chunks, finish, 0)


def on_device(coefficients, transfer_blocks):
    coef = coefficients[0, 0]
    blocks = transfer_blocks.reshape((transfer_blocks.shape[0],) + transfer_blocks.shape[3:])
    levels, rank, _ = blocks.shape
    total = coef.shape[1]
    chunks = total // WIDTH
    high_top = lax.axis_size("gx").bit_length() - 2
    low_top = lax.axis_size("gy").bit_length() - 2
    plan = [("gx", high_top), ("gy", low_top), ("gx", high_top - 1), ("gy", low_top - 1)]
    slots = (levels, chunks, rank, WIDTH)
    out = pl.pallas_call(
        functools.partial(kernel, plan),
        out_shape=jax.ShapeDtypeStruct(coef.shape, jnp.float32),
        in_specs=[pl.BlockSpec(memory_space=pl.ANY)] * 2,
        out_specs=pl.BlockSpec(memory_space=pl.ANY),
        scratch_shapes=[
            pltpu.VMEM(slots, jnp.float32),
            pltpu.VMEM(slots, jnp.float32),
            pltpu.VMEM(blocks.shape, jnp.float32),
            pltpu.VMEM((levels, 2, rank, 3 * rank), jnp.bfloat16),
            pltpu.VMEM(slots[1:], jnp.float32),
            pltpu.SemaphoreType.DMA((chunks,)),
            pltpu.SemaphoreType.DMA((levels,)),
            pltpu.SemaphoreType.DMA((chunks,)),
            pltpu.SemaphoreType.DMA((levels, chunks)),
            pltpu.SemaphoreType.DMA((levels, chunks)),
        ],
        compiler_params=pltpu.CompilerParams(
            collective_id=0, has_side_effects=True, vmem_limit_bytes=40 * 1024 * 1024
        ),
        cost_estimate=pl.CostEstimate(
            flops=12 * levels * rank * rank * total,
            bytes_accessed=4 * (2 * coef.size + blocks.size),
            transcendentals=0,
        ),
    )(coef, blocks)
    return out[None, None]


def solution(mesh):
    in_specs = (P("gx", "gy", None, None), P(None, "gx", "gy", None, None))
    out_specs = P("gx", "gy", None, None)
    return jax.shard_map(
        on_device, mesh=mesh, in_specs=in_specs, out_specs=out_specs, check_vma=False
    )
```

```python
import functools

import jax
import jax.numpy as jnp
from jax import lax
from jax.experimental import pallas as pl
from jax.experimental.pallas import tpu as pltpu
from jax.sharding import PartitionSpec as P

MESH = pl.DeviceIdType.MESH
WIDTH = 128
LAG = (0, 2, 3, 5)
AHEAD = 2


def high_low(x):
    high = x.astype(jnp.bfloat16)
    low = (x - high.astype(jnp.float32)).astype(jnp.bfloat16)
    return high, low


def right_side(x):
    high, low = high_low(x)
    return jnp.concatenate([high, low, high], axis=0)


def product(left, x):
    return jnp.dot(left, right_side(x), preferred_element_type=jnp.float32)


def kernel(plan, coef, blocks, out, state, got, raw, left, result,
           coef_sem, raw_sem, out_sem, send_sem, recv_sem):
    levels, chunks, rank, width = state.shape
    position = {"gx": lax.axis_index("gx"), "gy": lax.axis_index("gy")}
    upper, partner = [], []
    for axis, bit in plan:
        at = position[axis]
        one = lax.rem(at // (1 << bit), 2)
        upper.append(one)
        there = at + (1 - 2 * one) * (1 << bit)
        partner.append(
            (there, position["gy"]) if axis == "gx" else (position["gx"], there)
        )

    def columns(c):
        return pl.ds(pl.multiple_of(c * width, width), width)

    def load(c):
        return pltpu.make_async_copy(coef.at[:, columns(c)], state.at[0, c], coef_sem.at[c])

    def load_blocks(l):
        return pltpu.make_async_copy(blocks.at[l], raw.at[l], raw_sem.at[l])

    def send(l, c):
        return pltpu.make_async_remote_copy(
            src_ref=state.at[l, c],
            dst_ref=got.at[l, c],
            send_sem=send_sem.at[l, c],
            recv_sem=recv_sem.at[l, c],
            device_id=partner[l],
            device_id_type=MESH,
        )

    def store(c):
        return pltpu.make_async_copy(result.at[c], out.at[:, columns(c)], out_sem.at[c])

    for c in range(chunks):
        load(c).start()
    for l in range(levels):
        load_blocks(l).start()

    barrier = pltpu.get_barrier_semaphore()
    for l in range(levels):
        pl.semaphore_signal(barrier, inc=1, device_id=partner[l], device_id_type=MESH)
    pl.semaphore_wait(barrier, levels)

    def prepare(l):
        load_blocks(l).wait()
        for j in range(2):
            half = upper[l] if j == 0 else 1 - upper[l]
            part = raw[l, :, pl.ds(pl.multiple_of(half * rank, rank), rank)]
            high, low = high_low(part)
            left[l, j] = jnp.concatenate([high, high, low], axis=1)

    for c in range(chunks):
        load(c).wait()
        if c < AHEAD:
            send(0, c).start()
    prepare(0)

    def stage(l, c):
        own = product(left[l, 0], state[l, c])
        send(l, c).wait_recv()
        new = own + product(left[l, 1], got[l, c])
        if l + 1 < levels:
            state[l + 1, c] = new
            send(l + 1, c).start()
        else:
            result[c] = new
            store(c).start()

    def tick(t, carry):
        for l in range(levels):
            c = t - LAG[l]

            @pl.when(jnp.logical_and(c >= 0, c < chunks))
            def _(l=l, c=c):
                stage(l, c)
                if l == 0 and AHEAD < chunks:

                    @pl.when(t + AHEAD < chunks)
                    def _():
                        send(0, t + AHEAD).start()

        for l in range(1, levels):
            pl.when(t == l - 1)(functools.partial(prepare, l))
        return carry

    lax.fori_loop(0, chunks + LAG[-1], tick, 0)

    def finish(c, carry):
        for l in range(levels):
            send(l, c).wait_send()
        store(c).wait()
        return carry

    lax.fori_loop(0, chunks, finish, 0)


def on_device(coefficients, transfer_blocks):
    coef = coefficients[0, 0]
    blocks = transfer_blocks.reshape((transfer_blocks.shape[0],) + transfer_blocks.shape[3:])
    levels, rank, _ = blocks.shape
    total = coef.shape[1]
    chunks = total // WIDTH
    high_top = lax.axis_size("gx").bit_length() - 2
    low_top = lax.axis_size("gy").bit_length() - 2
    plan = [("gx", high_top), ("gy", low_top), ("gx", high_top - 1), ("gy", low_top - 1)]
    slots = (levels, chunks, rank, WIDTH)
    out = pl.pallas_call(
        functools.partial(kernel, plan),
        out_shape=jax.ShapeDtypeStruct(coef.shape, jnp.float32),
        in_specs=[pl.BlockSpec(memory_space=pl.ANY)] * 2,
        out_specs=pl.BlockSpec(memory_space=pl.ANY),
        scratch_shapes=[
            pltpu.VMEM(slots, jnp.float32),
            pltpu.VMEM(slots, jnp.float32),
            pltpu.VMEM(blocks.shape, jnp.float32),
            pltpu.VMEM((levels, 2, rank, 3 * rank), jnp.bfloat16),
            pltpu.VMEM(slots[1:], jnp.float32),
            pltpu.SemaphoreType.DMA((chunks,)),
            pltpu.SemaphoreType.DMA((levels,)),
            pltpu.SemaphoreType.DMA((chunks,)),
            pltpu.SemaphoreType.DMA((levels, chunks)),
            pltpu.SemaphoreType.DMA((levels, chunks)),
        ],
        compiler_params=pltpu.CompilerParams(
            collective_id=0, has_side_effects=True, vmem_limit_bytes=60 * 1024 * 1024
        ),
        cost_estimate=pl.CostEstimate(
            flops=12 * levels * rank * rank * total,
            bytes_accessed=4 * (2 * coef.size + blocks.size),
            transcendentals=0,
        ),
    )(coef, blocks)
    return out[None, None]


def solution(mesh):
    in_specs = (P("gx", "gy", None, None), P(None, "gx", "gy", None, None))
    out_specs = P("gx", "gy", None, None)
    return jax.shard_map(
        on_device, mesh=mesh, in_specs=in_specs, out_specs=out_specs, check_vma=False
    )
```

```python
import functools

import jax
import jax.numpy as jnp
from jax import lax
from jax.experimental import pallas as pl
from jax.experimental.pallas import tpu as pltpu
from jax.sharding import PartitionSpec as P

MESH = pl.DeviceIdType.MESH
WIDTH = 128
LAG = (0, 2, 3, 5)
AHEAD = 2


def high_low(x):
    high = x.astype(jnp.bfloat16)
    low = (x - high.astype(jnp.float32)).astype(jnp.bfloat16)
    return high, low


def right_side(x):
    high, low = high_low(x)
    return jnp.concatenate([high, low, high], axis=0)


def product(left, x):
    return jnp.dot(left, right_side(x), preferred_element_type=jnp.float32)


def kernel(plan, coef, blocks, out, state, got, raw, left, result,
           coef_sem, raw_sem, out_sem, send_sem, recv_sem):
    levels, chunks, rank, width = state.shape
    position = {"gx": lax.axis_index("gx"), "gy": lax.axis_index("gy")}
    upper, partner = [], []
    for axis, bit in plan:
        at = position[axis]
        one = lax.rem(at // (1 << bit), 2)
        upper.append(one)
        there = at + (1 - 2 * one) * (1 << bit)
        partner.append(
            (there, position["gy"]) if axis == "gx" else (position["gx"], there)
        )

    def columns(c):
        return pl.ds(pl.multiple_of(c * width, width), width)

    def load(c):
        return pltpu.make_async_copy(coef.at[:, columns(c)], state.at[0, c], coef_sem.at[c])

    def load_blocks(l):
        return pltpu.make_async_copy(blocks.at[l], raw.at[l], raw_sem.at[l])

    def send(l, c):
        return pltpu.make_async_remote_copy(
            src_ref=state.at[l, c],
            dst_ref=got.at[l, c],
            send_sem=send_sem.at[l, c],
            recv_sem=recv_sem.at[l, c],
            device_id=partner[l],
            device_id_type=MESH,
        )

    def store(c):
        return pltpu.make_async_copy(result.at[c], out.at[:, columns(c)], out_sem.at[c])

    for c in range(chunks):
        load(c).start()
    for l in range(levels):
        load_blocks(l).start()

    barrier = pltpu.get_barrier_semaphore()
    for l in range(levels):
        pl.semaphore_signal(barrier, inc=1, device_id=partner[l], device_id_type=MESH)
    pl.semaphore_wait(barrier, levels)

    def prepare(l):
        load_blocks(l).wait()
        for j in range(2):
            half = upper[l] if j == 0 else 1 - upper[l]
            part = raw[l, :, pl.ds(pl.multiple_of(half * rank, rank), rank)]
            high, low = high_low(part)
            left[l, j] = jnp.concatenate([high, high, low], axis=1)

    for c in range(chunks):
        load(c).wait()
        if c < AHEAD:
            send(0, c).start()
    prepare(0)

    def stage(l, c):
        own = product(left[l, 0], state[l, c])
        send(l, c).wait_recv()
        new = own + product(left[l, 1], got[l, c])
        if l + 1 < levels:
            state[l + 1, c] = new
            send(l + 1, c).start()
        else:
            result[c] = new
            store(c).start()

    def tick(t, carry):
        for l in range(levels):
            c = t - LAG[l]

            @pl.when(jnp.logical_and(c >= 0, c < chunks))
            def _(l=l, c=c):
                stage(l, c)
                if l == 0 and AHEAD < chunks:

                    @pl.when(t + AHEAD < chunks)
                    def _():
                        send(0, t + AHEAD).start()

        for l in range(1, levels):
            pl.when(t == l - 1)(functools.partial(prepare, l))
        return carry

    lax.fori_loop(0, chunks + LAG[-1], tick, 0)

    def finish(c, carry):
        for l in range(levels):
            send(l, c).wait_send()
        store(c).wait()
        return carry

    lax.fori_loop(0, chunks, finish, 0)


def on_device(coefficients, transfer_blocks):
    coef = coefficients[0, 0]
    blocks = transfer_blocks.reshape((transfer_blocks.shape[0],) + transfer_blocks.shape[3:])
    levels, rank, _ = blocks.shape
    total = coef.shape[1]
    chunks = total // WIDTH
    high_top = lax.axis_size("gx").bit_length() - 2
    low_top = lax.axis_size("gy").bit_length() - 2
    plan = [("gx", high_top), ("gy", low_top), ("gx", high_top - 1), ("gy", low_top - 1)]
    slots = (levels, chunks, rank, WIDTH)
    out = pl.pallas_call(
        functools.partial(kernel, plan),
        out_shape=jax.ShapeDtypeStruct(coef.shape, jnp.float32),
        in_specs=[pl.BlockSpec(memory_space=pl.ANY)] * 2,
        out_specs=pl.BlockSpec(memory_space=pl.ANY),
        scratch_shapes=[
            pltpu.VMEM(slots, jnp.float32),
            pltpu.VMEM(slots, jnp.float32),
            pltpu.VMEM(blocks.shape, jnp.float32),
            pltpu.VMEM((levels, 2, rank, 3 * rank), jnp.bfloat16),
            pltpu.VMEM(slots[1:], jnp.float32),
            pltpu.SemaphoreType.DMA((chunks,)),
            pltpu.SemaphoreType.DMA((levels,)),
            pltpu.SemaphoreType.DMA((chunks,)),
            pltpu.SemaphoreType.DMA((levels, chunks)),
            pltpu.SemaphoreType.DMA((levels, chunks)),
        ],
        compiler_params=pltpu.CompilerParams(
            collective_id=0, has_side_effects=True, vmem_limit_bytes=52 * 1024 * 1024
        ),
        cost_estimate=pl.CostEstimate(
            flops=12 * levels * rank * rank * total,
            bytes_accessed=4 * (2 * coef.size + blocks.size),
            transcendentals=0,
        ),
    )(coef, blocks)
    return out[None, None]


def solution(mesh):
    in_specs = (P("gx", "gy", None, None), P(None, "gx", "gy", None, None))
    out_specs = P("gx", "gy", None, None)
    return jax.shard_map(
        on_device, mesh=mesh, in_specs=in_specs, out_specs=out_specs, check_vma=False
    )
```

```python
import functools

import jax
import jax.numpy as jnp
from jax import lax
from jax.experimental import pallas as pl
from jax.experimental.pallas import tpu as pltpu
from jax.sharding import PartitionSpec as P

MESH = pl.DeviceIdType.MESH
WIDTH = 128
LAG = (0, 2, 3, 5)
AHEAD = 2


def high_low(x):
    high = x.astype(jnp.bfloat16)
    low = (x - high.astype(jnp.float32)).astype(jnp.bfloat16)
    return high, low


def right_side(x):
    high, low = high_low(x)
    return jnp.concatenate([high, low, high], axis=0)


def product(left, x):
    return jnp.dot(left, right_side(x), preferred_element_type=jnp.float32)


def kernel(plan, coef, blocks, out, state, got, raw, left, result,
           coef_sem, raw_sem, out_sem, send_sem, recv_sem):
    levels, chunks, rank, width = state.shape
    position = {"gx": lax.axis_index("gx"), "gy": lax.axis_index("gy")}
    upper, partner = [], []
    for axis, bit in plan:
        at = position[axis]
        one = lax.rem(at // (1 << bit), 2)
        upper.append(one)
        there = at + (1 - 2 * one) * (1 << bit)
        partner.append(
            (there, position["gy"]) if axis == "gx" else (position["gx"], there)
        )

    def columns(c):
        return pl.ds(pl.multiple_of(c * width, width), width)

    def load(c):
        return pltpu.make_async_copy(coef.at[:, columns(c)], state.at[0, c], coef_sem.at[c])

    def load_blocks(l):
        return pltpu.make_async_copy(blocks.at[l], raw.at[l], raw_sem.at[l])

    def send(l, c):
        return pltpu.make_async_remote_copy(
            src_ref=state.at[l, c],
            dst_ref=got.at[l, c],
            send_sem=send_sem.at[l, c],
            recv_sem=recv_sem.at[l, c],
            device_id=partner[l],
            device_id_type=MESH,
        )

    def store(c):
        return pltpu.make_async_copy(result.at[c], out.at[:, columns(c)], out_sem.at[c])

    barrier = pltpu.get_barrier_semaphore()
    for l in range(levels):
        pl.semaphore_signal(barrier, inc=1, device_id=partner[l], device_id_type=MESH)
    for c in range(chunks):
        load(c).start()
    for l in range(levels):
        load_blocks(l).start()
    pl.semaphore_wait(barrier, levels)

    def prepare(l):
        load_blocks(l).wait()
        for j in range(2):
            half = upper[l] if j == 0 else 1 - upper[l]
            part = raw[l, :, pl.ds(pl.multiple_of(half * rank, rank), rank)]
            high, low = high_low(part)
            left[l, j] = jnp.concatenate([high, high, low], axis=1)

    for c in range(AHEAD):
        load(c).wait()
        send(0, c).start()
    prepare(0)
    for c in range(AHEAD, chunks):
        load(c).wait()

    def stage(l, c):
        own = product(left[l, 0], state[l, c])
        send(l, c).wait_recv()
        new = own + product(left[l, 1], got[l, c])
        if l + 1 < levels:
            state[l + 1, c] = new
            send(l + 1, c).start()
        else:
            result[c] = new
            store(c).start()

    def tick(t, carry):
        for l in range(levels):
            c = t - LAG[l]

            @pl.when(jnp.logical_and(c >= 0, c < chunks))
            def _(l=l, c=c):
                stage(l, c)
                if l == 0 and AHEAD < chunks:

                    @pl.when(t + AHEAD < chunks)
                    def _():
                        send(0, t + AHEAD).start()

        for l in range(1, levels):
            pl.when(t == l - 1)(functools.partial(prepare, l))
        return carry

    lax.fori_loop(0, chunks + LAG[-1], tick, 0)

    def finish(c, carry):
        for l in range(levels):
            send(l, c).wait_send()
        store(c).wait()
        return carry

    lax.fori_loop(0, chunks, finish, 0)


def on_device(coefficients, transfer_blocks):
    coef = coefficients[0, 0]
    blocks = transfer_blocks.reshape((transfer_blocks.shape[0],) + transfer_blocks.shape[3:])
    levels, rank, _ = blocks.shape
    total = coef.shape[1]
    chunks = total // WIDTH
    high_top = lax.axis_size("gx").bit_length() - 2
    low_top = lax.axis_size("gy").bit_length() - 2
    plan = [("gx", high_top), ("gy", low_top), ("gx", high_top - 1), ("gy", low_top - 1)]
    slots = (levels, chunks, rank, WIDTH)
    out = pl.pallas_call(
        functools.partial(kernel, plan),
        out_shape=jax.ShapeDtypeStruct(coef.shape, jnp.float32),
        in_specs=[pl.BlockSpec(memory_space=pl.ANY)] * 2,
        out_specs=pl.BlockSpec(memory_space=pl.ANY),
        scratch_shapes=[
            pltpu.VMEM(slots, jnp.float32),
            pltpu.VMEM(slots, jnp.float32),
            pltpu.VMEM(blocks.shape, jnp.float32),
            pltpu.VMEM((levels, 2, rank, 3 * rank), jnp.bfloat16),
            pltpu.VMEM(slots[1:], jnp.float32),
            pltpu.SemaphoreType.DMA((chunks,)),
            pltpu.SemaphoreType.DMA((levels,)),
            pltpu.SemaphoreType.DMA((chunks,)),
            pltpu.SemaphoreType.DMA((levels, chunks)),
            pltpu.SemaphoreType.DMA((levels, chunks)),
        ],
        compiler_params=pltpu.CompilerParams(
            collective_id=0, has_side_effects=True, vmem_limit_bytes=52 * 1024 * 1024
        ),
        cost_estimate=pl.CostEstimate(
            flops=12 * levels * rank * rank * total,
            bytes_accessed=4 * (2 * coef.size + blocks.size),
            transcendentals=0,
        ),
    )(coef, blocks)
    return out[None, None]


def solution(mesh):
    in_specs = (P("gx", "gy", None, None), P(None, "gx", "gy", None, None))
    out_specs = P("gx", "gy", None, None)
    return jax.shard_map(
        on_device, mesh=mesh, in_specs=in_specs, out_specs=out_specs, check_vma=False
    )
```
